32 devices in a mesh: rec: 4 (over z), tm: 8 (over y, x, core).
Axes of the slice: x: 2, y: 2, z: 4, core: 2. Of those that a mesh axis runs over, the one named last changes fastest.
Arguments:
- frames: bfloat16 [8192, 1280], P(('rec', 'tm')), parts along dimension 0, may hold values from -50 to 50
- w_query: bfloat16 [1280, 1280], replicated, may hold values from -1 to 1
- w_kv: bfloat16 [1280, 2560], replicated, may hold values from -1 to 1
- w_out: bfloat16 [1280, 1280], replicated, may hold values from -0.15625 to 0.15625
- norm_gain: float32 [1280], replicated, may hold values from 0.5 to 1.5
- rand_owner: int32 [64, 3], P(('rec', 'tm')), parts along dimension 0, may hold values from 0 to 7, all different within a row; in each aligned block of 2 rows (0 to 1, 2 to 3, ...) at most 2 rows name the same one
- rand_slot: int32 [64, 3], P(('rec', 'tm')), parts along dimension 0, may hold values from 0 to 1
- global_pos: int32 [512], P('rec'), parts along dimension 0, may hold values from 0 to 2047
- length: int32 [4], P('rec'), parts along dimension 0, may hold values from 8 to 16
Outputs:
- pooled_out: bfloat16 [2048, 1280], P(('rec', 'tm')), parts along dimension 0
The draws below stay inside these ranges and needn't reach their ends.
There are 4 independent parts, one for each index of `rec`. The reference program is written for one: setup_inputs(seed, part) draws one part's arguments, and reference() takes and returns one part's arrays. A program takes and returns all parts, laid end to end along the dimension named above; an argument that names none is the same for every part. Nothing has to cross between parts.
Inputs may be any that keep to these rules, and one draw needn't show every extreme that they name: `rand_owner`: the 3 owners of one query block differ; over the query blocks of one time shard no owner is named more than 2 times, a bound that some block reaches.
All inputs are finite; a program needn't handle non-finite values.
Results may differ from the reference program's by a relative error of at most 0.012.
The reference program's roundings to bfloat16 on the way count: a program that leaves them out, or rounds other values in their place, can miss the bound.
Values may be sent and summed in bfloat16 or wider, within the bound.
A program may use at most 128 MiB of HBM per device.

```python
import math
import jax
import jax.numpy as jnp
import numpy as np
from jax import lax

D = 1280
HEADS = 20
BLOCK = 128
PICKS = 3
POOL = 4
GLOBALS = 128
QB_DEV = 2
SHARDS = 8
QBLOCKS = 16
FRAMES = 2048
CAP = 2


def draw_frames(key, part):
    normal_draw = jnp.clip(jax.random.normal(jax.random.fold_in(key, 31), (FRAMES, D), jnp.float32), -4.0, 4.0)
    return normal_draw.astype(jnp.bfloat16)


def query_base(key):
    return jnp.clip(jax.random.normal(jax.random.fold_in(key, 41), (D, D), jnp.float32), -4.0, 4.0) / jnp.sqrt(jnp.float32(D))


def draw_w_query(key, part):
    return query_base(key).astype(jnp.bfloat16)


def draw_w_kv(key, part):
    fresh_draw = jnp.clip(jax.random.normal(jax.random.fold_in(key, 42), (D, 2 * D), jnp.float32), -4.0, 4.0) / jnp.sqrt(jnp.float32(D))
    return fresh_draw.astype(jnp.bfloat16)


def draw_global_pos(key, part):
    shard_rows = QB_DEV * BLOCK
    spread_pos = jax.random.randint(jax.random.fold_in(key, 51), (GLOBALS,), 0, FRAMES, jnp.int32)
    home_shard = jax.random.randint(jax.random.fold_in(key, 52), (), 0, max(1, SHARDS // 2), jnp.int32)
    packed_pos = home_shard * shard_rows + jax.random.randint(jax.random.fold_in(key, 53), (GLOBALS,), 0, shard_rows, jnp.int32)
    return jnp.where(part % 4 == 0, packed_pos, spread_pos).astype(jnp.int32)


def set_ends(values, rng, smallest, high):
    shape = values.shape
    index_at = [jax.random.randint(jax.random.fold_in(rng, axis), (), 0, shape[axis]) for axis in range(len(shape))]
    values = values.at[tuple(index_at)].set(smallest)
    longest = shape.index(max(shape))
    index_at[longest] = (index_at[longest] + 1) % shape[longest]
    return values.at[tuple(index_at)].set(high)


def routed_block(stream_key, own, number, rows, number_of, top, bound, slope):
    ranking = jax.random.permutation(stream_key, number_of)
    heavy_load, ordinary = shares(number_of, rows * top, bound, slope, True), shares(number_of, rows * top, bound, slope, False)
    places = jnp.arange(number_of)

    def named(lengths, turn):
        used = int((lengths > 0).sum())
        fixed = max(1, used // 4)
        moved = fixed + (places - fixed + turn * (used - fixed)) % max(1, number_of - fixed)
        return jnp.zeros((number_of,), jnp.int32).at[ranking[jnp.where(places < fixed, places, moved)]].set(jnp.asarray(lengths, jnp.int32))

    lengths = jnp.where(number % 4 == 0, named(heavy_load, number // 4), named(ordinary, number - number // 4 - 1))
    mixed = jax.random.permutation(jax.random.fold_in(own, 3), number_of)
    giver, sink = mixed[0:number_of // 2 * 2:2], mixed[1:number_of // 2 * 2:2]
    room = jnp.minimum(lengths[giver] - 1, bound - lengths[sink]) // 2
    room = jnp.where((giver == ranking[0]) | (sink == ranking[0]) | (lengths[sink] == 0), 0, jnp.maximum(room, 0))
    moved = jax.random.randint(jax.random.fold_in(own, 4), (number_of // 2,), 0, 1 << 20) % (room + 1)
    lengths = lengths.at[giver].add(-moved).at[sink].add(moved)
    items = jnp.searchsorted(jnp.cumsum(lengths), jnp.arange(rows * top), side="right").astype(jnp.int32)
    table = items.reshape(top, rows).T
    table = table[jax.random.permutation(jax.random.fold_in(own, 1), rows)]
    turn = jax.random.randint(jax.random.fold_in(own, 2), (rows, 1), 0, top)
    return jnp.take_along_axis(table, (jnp.arange(top)[None, :] + turn) % top, axis=1)


def shares(count, total, bound, skew, full):
    loads = [(1 << 20) // math.isqrt(rank ** skew) + 1 for rank in range(1, count + 1)]
    largest = bound if full else min(bound, max(-(-total // count), total * loads[0] // sum(loads)))
    least = 1 if total - largest >= count - 1 else 0
    given, spare = [largest] + [least] * (count - 1), total - largest - least * (count - 1)
    while spare > 0:
        movable = [i for i in range(1, count) if given[i] < largest] or [i for i in range(1, count) if given[i] < bound]
        mass, left = sum([loads[i] for i in movable]), spare
        for i in movable:
            more = min(bound - given[i], max(1, left * loads[i] // mass), spare)
            given[i] = given[i] + more
            spare = spare - more
    return np.array(given)


def scatter_about(own_key, dims, width, most, held_as=jnp.bfloat16):
    values = width * jax.random.normal(own_key, dims, jnp.float32)
    return jnp.clip(values, min=-most, max=most).astype(held_as)


def setup_inputs(seed: int = 0, part: int = 0) -> dict:
    splits = jax.random.split(jax.random.key(seed), 10)
    own_keys = jax.random.split(jax.random.fold_in(splits[9], part), 10)
    frames = draw_frames(jax.random.fold_in(jax.random.fold_in(splits[9], part), 71), part)
    w_query = draw_w_query(jax.random.fold_in(splits[9], 71), part)
    w_kv = draw_w_kv(jax.random.fold_in(splits[9], 71), part)
    w_out = scatter_about(splits[3], (D, D), D ** -0.5, 0.15625)
    norm_gain = jnp.clip(1.0 + 0.1 * jax.random.normal(splits[4], (D,), jnp.float32), 0.5, 1.5)
    rand_owner_keys = jax.random.split(jax.random.fold_in(own_keys[5], 1), QBLOCKS // QB_DEV)
    rand_owner_turns = jax.random.permutation(jax.random.fold_in(own_keys[5], 3), QBLOCKS // QB_DEV)
    rand_owner = jax.vmap(lambda own, number: routed_block(jax.random.fold_in(own_keys[5], 2), own, number, QB_DEV, SHARDS, PICKS, CAP, 2))(rand_owner_keys, rand_owner_turns).reshape((QBLOCKS, PICKS))
    rand_slot = set_ends(jax.random.randint(own_keys[6], (QBLOCKS, PICKS), 0, QB_DEV), jax.random.fold_in(own_keys[6], 1), 0, QB_DEV - 1).astype(jnp.int32)
    global_pos = draw_global_pos(jax.random.fold_in(jax.random.fold_in(splits[9], part), 71), part)
    length = jax.random.randint(own_keys[8], (1,), QBLOCKS // 2, QBLOCKS + 1).astype(jnp.int32)
    return {"frames": frames, "w_query": w_query, "w_kv": w_kv, "w_out": w_out, "norm_gain": norm_gain, "rand_owner": rand_owner, "rand_slot": rand_slot, "global_pos": global_pos, "length": length}


def attend(query_rows, key_rows, key_live, global_keys, global_live, head_count):
    group_size, block_rows, model_width = query_rows.shape
    head_size = model_width // head_count
    score_scale = head_size ** (-0.5)
    query_h = query_rows.astype(jnp.float32).reshape(group_size, block_rows, head_count, head_size)
    key_h = key_rows[..., :model_width].astype(jnp.float32).reshape(group_size, -1, head_count, head_size)
    value_h = key_rows[..., model_width:].astype(jnp.float32).reshape(group_size, -1, head_count, head_size)
    global_key_h = global_keys[:, :model_width].astype(jnp.float32).reshape(-1, head_count, head_size)
    global_value_h = global_keys[:, model_width:].astype(jnp.float32).reshape(-1, head_count, head_size)
    near_scores = jnp.einsum('bihd,bjhd->bhij', query_h, key_h) * score_scale
    far_scores = jnp.einsum('bihd,jhd->bhij', query_h, global_key_h) * score_scale
    near_scores = jnp.where(key_live[:, None, None, :], near_scores, -1e+30)
    far_scores = jnp.where(global_live[None, None, None, :], far_scores, -1e+30)
    row_max = jnp.maximum(lax.optimization_barrier(jnp.max(near_scores, axis=-1)), lax.optimization_barrier(jnp.max(far_scores, axis=-1)))[..., None]
    near_exp = jnp.exp(near_scores - row_max)
    far_exp = jnp.exp(far_scores - row_max)
    row_total = lax.optimization_barrier(jnp.sum(near_exp, axis=-1, keepdims=True)) + lax.optimization_barrier(jnp.sum(far_exp, axis=-1, keepdims=True))
    near_weight = (near_exp / row_total).astype(jnp.bfloat16).astype(jnp.float32)
    far_weight = (far_exp / row_total).astype(jnp.bfloat16).astype(jnp.float32)
    context = jnp.einsum('bhij,bjhd->bihd', near_weight, value_h)
    context = context + jnp.einsum('bhij,jhd->bihd', far_weight, global_value_h)
    return context.reshape(group_size, block_rows, model_width).astype(jnp.bfloat16)

def reference(frames, w_query, w_kv, w_out, norm_gain, rand_owner, rand_slot, global_pos, length):
    model_width = frames.shape[1]
    query_rows = jnp.dot(frames, w_query, preferred_element_type=jnp.float32).astype(jnp.bfloat16)
    keyval = jnp.dot(frames, w_kv, preferred_element_type=jnp.float32).astype(jnp.bfloat16)
    live_blocks = length[0]
    zero_rim = jnp.zeros((BLOCK, 2 * model_width), jnp.bfloat16)
    padded = jnp.concatenate([zero_rim, keyval, zero_rim], axis=0)
    kv_blocks = keyval.reshape(QBLOCKS, BLOCK, 2 * model_width)
    global_keys = jnp.take(keyval, global_pos, axis=0)
    global_live = global_pos < live_blocks * BLOCK
    random_ids = (rand_owner * QB_DEV + rand_slot).astype(jnp.int32)

    def one_block(index):
        window = lax.dynamic_slice_in_dim(padded, index * BLOCK, 3 * BLOCK, 0)
        picked = jnp.take(kv_blocks, random_ids[index], axis=0).reshape(PICKS * BLOCK, 2 * model_width)
        key_rows = jnp.concatenate([window, picked], axis=0)[None]
        block_ids = jnp.concatenate([index - 1 + jnp.arange(3, dtype=jnp.int32), random_ids[index]])
        key_live = jnp.repeat((block_ids >= 0) & (block_ids < live_blocks), BLOCK)[None]
        rows_here = lax.dynamic_slice_in_dim(query_rows, index * BLOCK, BLOCK, 0)[None]
        return attend(rows_here, key_rows, key_live, global_keys, global_live, HEADS)[0]
    context = lax.map(one_block, jnp.arange(QBLOCKS, dtype=jnp.int32)).reshape(FRAMES, model_width)
    projected = jnp.dot(context, w_out, preferred_element_type=jnp.float32)
    pooled = lax.optimization_barrier(jnp.mean(projected.reshape(FRAMES // POOL, POOL, model_width), axis=1))
    feature_mean = lax.optimization_barrier(jnp.mean(pooled, axis=1, keepdims=True))
    centered = pooled - feature_mean
    feature_var = lax.optimization_barrier(jnp.mean(centered * centered, axis=1, keepdims=True))
    normed = centered * lax.rsqrt(feature_var + 1e-05) * norm_gain
    row_block = jnp.arange(FRAMES // POOL, dtype=jnp.int32) * POOL // BLOCK
    return jnp.where((row_block < live_blocks)[:, None], normed, 0.0).astype(jnp.bfloat16)
```

```python
import functools

import jax
import jax.numpy as jnp
from jax import lax
from jax.experimental import pallas as pl
from jax.experimental.pallas import tpu as pltpu
from jax.sharding import PartitionSpec as P

HEADS = 20
BLOCK = 128
POOL = 4
TILE = 512
MESH = pl.DeviceIdType.MESH
F32 = jnp.float32
BF16 = jnp.bfloat16


def kernel(shards, frames, w_query, w_kv, w_out, gain, owner, slot, gpos, length, out,
           fall, kv, wq_v, wkv_v, wout_v, q_v, gacc, gkv, pctx, proj, lsem, ssem, rsem, psem):
    me = lax.axis_index("tm")
    width = wq_v.shape[0]
    picks = owner.shape[1]
    first = me * 2
    count = [0]
    sends = []

    def local(src, dst, index):
        copy = pltpu.make_async_copy(src, dst, lsem.at[index])
        copy.start()
        return copy

    def send(src, shard, part, target):
        copy = pltpu.make_async_remote_copy(
            src_ref=src, dst_ref=fall.at[shard, part], send_sem=ssem.at[count[0]],
            recv_sem=rsem.at[shard, part], device_id={"tm": target}, device_id_type=MESH)
        count[0] += 1
        copy.start()
        sends.append(copy)

    def arrived(shard, part):
        pltpu.make_async_copy(fall.at[shard, part], fall.at[shard, part],
                              rsem.at[shard, part]).wait()

    own = local(frames, fall.at[me], 0)
    got_q = local(w_query, wq_v, 1)
    got_kv = local(w_kv, wkv_v, 2)
    got_out = local(w_out, wout_v, 3)

    if shards == 8:
        side = me + 1 - 2 * (me % 2)
        near_x = me + 2 - 4 * ((me // 2) % 2)
        near_y = (me + 4) % 8
        partners = [side, near_x, near_y]
    else:
        partners = [(me + k) % shards for k in range(1, shards)]
    barrier = pltpu.get_barrier_semaphore()
    for target in partners:
        pl.semaphore_signal(barrier, inc=1, device_id={"tm": target}, device_id_type=MESH)
    pl.semaphore_wait(barrier, len(partners))
    if shards == 8:
        send(frames.at[0], me, 0, near_x)
        send(frames.at[1], me, 1, near_y)
        send(frames.at[1], me, 1, near_x)
        send(frames.at[0], me, 0, near_y)
        send(frames.at[0], me, 0, side)
        send(frames.at[1], me, 1, side)
    else:
        for target in partners:
            send(frames.at[0], me, 0, target)
            send(frames.at[1], me, 1, target)

    gacc[...] = jnp.zeros_like(gacc)
    pos_t = jnp.broadcast_to(gpos[...], (BLOCK, BLOCK)).T
    lane = lax.broadcasted_iota(jnp.int32, (BLOCK, BLOCK), 1)

    def onehot(block):
        return jnp.where(pos_t == block * BLOCK + lane, 1.0, 0.0).astype(BF16)

    def project(shard_a, part_a, shard_b, part_b):
        block_a, block_b = shard_a * 2 + part_a, shard_b * 2 + part_b
        hot = jnp.concatenate([onehot(block_a), onehot(block_b)], axis=1)

        def step(n, carry):
            cols = pl.ds(pl.multiple_of(n * TILE, TILE), TILE)
            rows = jnp.concatenate([fall[shard_a, part_a], fall[shard_b, part_b]], axis=0)
            made = jnp.dot(rows, wkv_v[:, cols], preferred_element_type=F32).astype(BF16)
            kv[block_a, :, cols] = made[:BLOCK]
            kv[block_b, :, cols] = made[BLOCK:]
            gacc[:, cols] += jnp.dot(hot, made, preferred_element_type=F32)
            return carry

        lax.fori_loop(0, 2 * width // TILE, step, 0)

    own.wait()
    got_q.wait()

    def query_step(n, carry):
        cols = pl.ds(pl.multiple_of(n * 256, 256), 256)
        rows = jnp.concatenate([fall[me, 0], fall[me, 1]], axis=0)
        made = jnp.dot(rows, wq_v[:, cols], preferred_element_type=F32).astype(BF16)
        q_v[:, cols] = (made.astype(F32) * 0.125).astype(BF16)
        return carry

    lax.fori_loop(0, width // 256, query_step, 0)
    got_kv.wait()
    project(me, 0, me, 1)
    if shards == 8:
        diag = near_x + near_y - me
        side_x, side_y = (v + 1 - 2 * (v % 2) for v in (near_x, near_y))
        side_d = diag + 1 - 2 * (diag % 2)
        arrived(side, 0)
        arrived(side, 1)
        project(side, 0, side, 1)
        arrived(near_x, 0)
        send(fall.at[near_x, 0], near_x, 0, near_y)
        send(fall.at[near_x, 0], near_x, 0, side)
        arrived(near_y, 1)
        send(fall.at[near_y, 1], near_y, 1, near_x)
        send(fall.at[near_y, 1], near_y, 1, side)
        project(near_x, 0, near_y, 1)
        arrived(side_x, 0)
        arrived(side_y, 1)
        project(side_x, 0, side_y, 1)
        arrived(near_x, 1)
        send(fall.at[near_x, 1], near_x, 1, side)
        arrived(near_y, 0)
        send(fall.at[near_y, 0], near_y, 0, side)
        project(near_x, 1, near_y, 0)
        arrived(side_x, 1)
        arrived(side_y, 0)
        project(side_x, 1, side_y, 0)
        arrived(diag, 0)
        send(fall.at[diag, 0], diag, 0, side)
        arrived(diag, 1)
        send(fall.at[diag, 1], diag, 1, side)
        project(diag, 0, diag, 1)
        arrived(side_d, 0)
        arrived(side_d, 1)
        project(side_d, 0, side_d, 1)
    else:
        for k in range(1, shards):
            source = (me + shards - k) % shards
            arrived(source, 0)
            arrived(source, 1)
            project(source, 0, source, 1)
    gkv[...] = gacc[...].astype(BF16)

    live = length[0]
    low = jnp.where(lane < 64, 1.0, 0.0).astype(BF16)
    high = jnp.where(lane < 64, 0.0, 1.0).astype(BF16)
    pool_row = lax.broadcasted_iota(jnp.int32, (BLOCK // POOL, BLOCK), 0)
    pool_col = lax.broadcasted_iota(jnp.int32, (BLOCK // POOL, BLOCK), 1)
    pool = jnp.where(pool_col // POOL == pool_row, 1.0 / POOL, 0.0).astype(BF16)
    far_bias = jnp.where(gpos[...] < live * BLOCK, 0.0, -1e30)
    blocks, biases = [], []
    for b in range(2):
        ids = [first + b - 1 + k for k in range(3)]
        ids += [owner[b, j] * 2 + slot[b, j] for j in range(picks)]
        blocks.append([jnp.clip(i, 0, 2 * shards - 1) for i in ids])
        row = [jnp.full((1, BLOCK), jnp.where((i >= 0) & (i < live), 0.0, -1e30), F32) for i in ids]
        biases.append(jnp.concatenate(row + [far_bias], axis=1))

    def pair_step(p, carry):
        kcols = pl.ds(pl.multiple_of(p * 128, 128), 128)
        vcols = pl.ds(pl.multiple_of(width + p * 128, 128), 128)
        for b in range(2):
            q = q_v[b * BLOCK:(b + 1) * BLOCK, kcols]
            qs = jnp.concatenate([q * low, q * high], axis=0)
            keys = jnp.concatenate([kv[i, :, kcols] for i in blocks[b]] + [gkv[:, kcols]], axis=0)
            vals = jnp.concatenate([kv[i, :, vcols] for i in blocks[b]] + [gkv[:, vcols]], axis=0)
            s = lax.dot_general(qs, keys, (((1,), (1,)), ((), ())), preferred_element_type=F32)
            s = s + biases[b]
            e = jnp.exp(s - jnp.max(s, axis=1, keepdims=True))
            total = jnp.sum(e, axis=1, keepdims=True)
            o = jnp.dot(e.astype(BF16), vals, preferred_element_type=F32) / total
            c = jnp.where(lane < 64, o[:BLOCK], o[BLOCK:]).astype(BF16)
            pctx[b * 32:(b + 1) * 32, kcols] = jnp.dot(pool, c, preferred_element_type=F32)
        return carry

    lax.fori_loop(0, width // 128, pair_step, 0)
    got_out.wait()
    rows = pctx.shape[0]
    upper = pctx[...].astype(BF16)
    lower = (pctx[...] - upper.astype(F32)).astype(BF16)
    both = jnp.concatenate([upper, lower], axis=0)
    for n in range(width // 256):
        made = jnp.dot(both, wout_v[:, n * 256:(n + 1) * 256], preferred_element_type=F32)
        proj[:, n * 256:(n + 1) * 256] = made[:rows] + made[rows:]
    pooled = proj[...]
    centered = pooled - jnp.mean(pooled, axis=1, keepdims=True)
    var = jnp.mean(centered * centered, axis=1, keepdims=True)
    normed = centered * lax.rsqrt(var + 1e-05) * gain[...]
    row_block = first + lax.broadcasted_iota(jnp.int32, (rows, width), 0) * POOL // BLOCK
    out[...] = jnp.where(row_block < live, normed, 0.0).astype(BF16)
    for copy in sends:
        copy.wait_send()


def body(shards, frames, w_query, w_kv, w_out, norm_gain, rand_owner, rand_slot, global_pos, length):
    local_rows, width = frames.shape
    assert local_rows == 2 * BLOCK and width == HEADS * 64 and global_pos.shape[0] == BLOCK
    hbm = pl.BlockSpec(memory_space=pl.ANY)
    vmem = pl.BlockSpec(memory_space=pltpu.VMEM)
    smem = pl.BlockSpec(memory_space=pltpu.SMEM)
    n_sends = 14 if shards == 8 else 2 * (shards - 1)
    return pl.pallas_call(
        functools.partial(kernel, shards),
        out_shape=jax.ShapeDtypeStruct((local_rows // POOL, width), BF16),
        in_specs=[hbm, hbm, hbm, hbm, vmem, smem, smem, vmem, smem],
        out_specs=vmem,
        scratch_shapes=[
            pltpu.VMEM((shards, 2, BLOCK, width), BF16),
            pltpu.VMEM((2 * shards, BLOCK, 2 * width), BF16),
            pltpu.VMEM((width, width), BF16),
            pltpu.VMEM((width, 2 * width), BF16),
            pltpu.VMEM((width, width), BF16),
            pltpu.VMEM((local_rows, width), BF16),
            pltpu.VMEM((BLOCK, 2 * width), F32),
            pltpu.VMEM((BLOCK, 2 * width), BF16),
            pltpu.VMEM((local_rows // POOL, width), F32),
            pltpu.VMEM((local_rows // POOL, width), F32),
            pltpu.SemaphoreType.DMA((4,)),
            pltpu.SemaphoreType.DMA((n_sends,)),
            pltpu.SemaphoreType.DMA((shards, 2)),
            pltpu.SemaphoreType.DMA((1,)),
        ],
        compiler_params=pltpu.CompilerParams(
            collective_id=0, has_side_effects=True, vmem_limit_bytes=60 * 1024 * 1024),
        cost_estimate=pl.CostEstimate(
            flops=20_000_000_000, bytes_accessed=20_000_000, transcendentals=5_000_000),
    )(frames.reshape(2, BLOCK, width), w_query, w_kv, w_out, norm_gain.reshape(1, width),
      rand_owner, rand_slot, global_pos.reshape(1, BLOCK), length)


def solution(mesh):
    placed = (
        P(("rec", "tm"), None), P(), P(), P(), P(),
        P(("rec", "tm"), None), P(("rec", "tm"), None), P("rec"), P("rec"),
    )
    return jax.shard_map(
        functools.partial(body, mesh.shape["tm"]), mesh=mesh, in_specs=placed,
        out_specs=P(("rec", "tm"), None), check_vma=False)
```

```python
import functools

import jax
import jax.numpy as jnp
from jax import lax
from jax.experimental import pallas as pl
from jax.experimental.pallas import tpu as pltpu
from jax.sharding import PartitionSpec as P

HEADS = 20
BLOCK = 128
POOL = 4
TILE = 256
MESH = pl.DeviceIdType.MESH
F32 = jnp.float32
BF16 = jnp.bfloat16


def kernel(shards, frames, w_query, w_kv, w_out, gain, owner, slot, gpos, length, out,
           fall, kv, wq_v, wkv_v, wout_v, q_v, gacc, gkv, pctx, proj, s_a, s_b, m_a, m_b, lsem, ssem, rsem, kssem, krsem):
    me = lax.axis_index("tm")
    width = wq_v.shape[0]
    picks = owner.shape[1]
    first = me * 2
    count = [0]
    sends = []

    def local(src, dst, index):
        copy = pltpu.make_async_copy(src, dst, lsem.at[index])
        copy.start()
        return copy

    def send(src, shard, part, target):
        copy = pltpu.make_async_remote_copy(
            src_ref=src, dst_ref=fall.at[shard, part], send_sem=ssem.at[count[0]],
            recv_sem=rsem.at[shard, part], device_id={"tm": target}, device_id_type=MESH)
        count[0] += 1
        copy.start()
        sends.append(copy)

    def arrived(shard, part):
        pltpu.make_async_copy(fall.at[shard, part], fall.at[shard, part],
                              rsem.at[shard, part]).wait()

    own = local(frames, fall.at[me], 0)
    got_q = local(w_query, wq_v, 1)
    got_kv = local(w_kv, wkv_v, 2)
    got_out = local(w_out, wout_v, 3)

    if shards == 8:
        side = me + 1 - 2 * (me % 2)
        near_x = me + 2 - 4 * ((me // 2) % 2)
        near_y = (me + 4) % 8
        partners = [side, near_x, near_y]
    else:
        partners = [(me + k) % shards for k in range(1, shards)]
    barrier = pltpu.get_barrier_semaphore()
    for target in partners:
        pl.semaphore_signal(barrier, inc=1, device_id={"tm": target}, device_id_type=MESH)
    pl.semaphore_wait(barrier, len(partners))
    if shards == 8:
        send(frames.at[0], me, 0, near_x)
        send(frames.at[1], me, 1, near_y)
        send(frames.at[1], me, 1, near_x)
        send(frames.at[0], me, 0, near_y)
    else:
        for target in partners:
            send(frames.at[0], me, 0, target)
            send(frames.at[1], me, 1, target)

    gacc[...] = jnp.zeros_like(gacc)
    pos_t = jnp.broadcast_to(gpos[...], (BLOCK, BLOCK)).T
    lane = lax.broadcasted_iota(jnp.int32, (BLOCK, BLOCK), 1)

    def onehot(block):
        return jnp.where(pos_t == block * BLOCK + lane, 1.0, 0.0).astype(BF16)

    passed = []

    def pass_on(block, n):
        part = kv.at[block, pl.ds(n * 2, 2)]
        return pltpu.make_async_remote_copy(
            src_ref=part, dst_ref=part, send_sem=kssem.at[block, n], recv_sem=krsem.at[block, n],
            device_id={"tm": side}, device_id_type=MESH)

    def add_global(n, hot, keys, vals_t):
        far_k = jnp.dot(hot, keys, preferred_element_type=F32)
        far_v = lax.dot_general(vals_t, hot, (((1,), (1,)), ((), ())), preferred_element_type=F32)
        for j in range(2):
            gacc[n * 2 + j, 0] += far_k[:, j * 128:(j + 1) * 128]
            gacc[n * 2 + j, 1] += far_v[j * 128:(j + 1) * 128]

    def project(shard_a, part_a, shard_b, part_b):
        block_a, block_b = shard_a * 2 + part_a, shard_b * 2 + part_b
        hot = jnp.concatenate([onehot(block_a), onehot(block_b)], axis=1)

        def step(n, carry):
            kcols = pl.ds(pl.multiple_of(n * TILE, TILE), TILE)
            vcols = pl.ds(pl.multiple_of(width + n * TILE, TILE), TILE)
            rows = jnp.concatenate([fall[shard_a, part_a], fall[shard_b, part_b]], axis=0)
            keys = jnp.dot(rows, wkv_v[:, kcols], preferred_element_type=F32).astype(BF16)
            vals_t = jnp.dot(rows, wkv_v[:, vcols], preferred_element_type=F32).T.astype(BF16)
            for k, block in enumerate((block_a, block_b)):
                for j in range(2):
                    kv[block, n * 2 + j, 0] = keys[k * 128:(k + 1) * 128, j * 128:(j + 1) * 128]
                    kv[block, n * 2 + j, 1] = vals_t[j * 128:(j + 1) * 128, k * 128:(k + 1) * 128]
            if shards == 8:
                pass_on(block_a, n).start()
                pass_on(block_b, n).start()
            add_global(n, hot, keys, vals_t)
            return carry

        lax.fori_loop(0, width // TILE, step, 0)
        if shards == 8:
            passed.append((block_a, block_b))

    def take(shard_a, part_a, shard_b, part_b):
        block_a, block_b = shard_a * 2 + part_a, shard_b * 2 + part_b
        hot = jnp.concatenate([onehot(block_a), onehot(block_b)], axis=1)

        def step(n, carry):
            pass_on(block_a, n).wait_recv()
            pass_on(block_b, n).wait_recv()
            keys = jnp.concatenate([jnp.concatenate(
                [kv[block, n * 2 + j, 0] for j in range(2)], axis=1)
                for block in (block_a, block_b)], axis=0)
            vals_t = jnp.concatenate([jnp.concatenate(
                [kv[block, n * 2 + j, 1] for block in (block_a, block_b)], axis=1)
                for j in range(2)], axis=0)
            add_global(n, hot, keys, vals_t)
            return carry

        lax.fori_loop(0, width // TILE, step, 0)

    own.wait()
    got_q.wait()

    def query_step(n, carry):
        cols = pl.ds(pl.multiple_of(n * 256, 256), 256)
        rows = jnp.concatenate([fall[me, 0], fall[me, 1]], axis=0)
        made = jnp.dot(rows, wq_v[:, cols], preferred_element_type=F32).astype(BF16)
        q_v[:, cols] = (made.astype(F32) * 0.125).astype(BF16)
        return carry

    lax.fori_loop(0, width // 256, query_step, 0)
    got_kv.wait()
    project(me, 0, me, 1)
    if shards == 8:
        diag = near_x + near_y - me
        side_x, side_y = (v + 1 - 2 * (v % 2) for v in (near_x, near_y))
        side_d = diag + 1 - 2 * (diag % 2)
        arrived(near_x, 0)
        send(fall.at[near_x, 0], near_x, 0, near_y)
        arrived(near_y, 1)
        send(fall.at[near_y, 1], near_y, 1, near_x)
        project(near_x, 0, near_y, 1)
        take(side, 0, side, 1)
        take(side_x, 0, side_y, 1)
        arrived(near_x, 1)
        arrived(near_y, 0)
        project(near_x, 1, near_y, 0)
        take(side_x, 1, side_y, 0)
        arrived(diag, 0)
        arrived(diag, 1)
        project(diag, 0, diag, 1)
        take(side_d, 0, side_d, 1)
    else:
        for k in range(1, shards):
            source = (me + shards - k) % shards
            arrived(source, 0)
            arrived(source, 1)
            project(source, 0, source, 1)
    gkv[...] = gacc[...].astype(BF16)

    live = length[0]
    low = jnp.where(lane < 64, 1.0, 0.0).astype(BF16)
    high = jnp.where(lane < 64, 0.0, 1.0).astype(BF16)
    pool_row = lax.broadcasted_iota(jnp.int32, (BLOCK // POOL, BLOCK), 0)
    pool_col = lax.broadcasted_iota(jnp.int32, (BLOCK // POOL, BLOCK), 1)
    pool = jnp.where(pool_col // POOL == pool_row, 1.0 / POOL, 0.0).astype(BF16)
    far = jnp.where(pos_t >= live * BLOCK, -1e30, 0.0)
    far = jnp.concatenate([far, far], axis=1)
    blocks, biases = [], []
    for b in range(2):
        ids = [first + b - 1 + k for k in range(3)]
        ids += [owner[b, j] * 2 + slot[b, j] for j in range(picks)]
        blocks.append([jnp.clip(i, 0, 2 * shards - 1) for i in ids])
        biases.append([jnp.where((i >= 0) & (i < live), 0.0, -1e30) for i in ids])

    pairs = width // 128

    def score(p, s_ref, m_ref):
        kcols = pl.ds(pl.multiple_of(p * 128, 128), 128)
        for b in range(2):
            q = q_v[b * BLOCK:(b + 1) * BLOCK, kcols]
            qs = jnp.concatenate([q * low, q * high], axis=0)
            keys = jnp.concatenate([kv[i, p, 0] for i in blocks[b]] + [gkv[p, 0]], axis=0)
            s = lax.dot_general(keys, qs, (((1,), (1,)), ((), ())), preferred_element_type=F32)
            near = [s[k * BLOCK:(k + 1) * BLOCK] + bias for k, bias in enumerate(biases[b])]
            s = jnp.concatenate(near + [s[len(near) * BLOCK:] + far], axis=0)
            s_ref[b] = s
            m_ref[b] = jnp.max(s, axis=0, keepdims=True)

    def combine(p, s_ref, m_ref):
        kcols = pl.ds(pl.multiple_of(p * 128, 128), 128)
        for b in range(2):
            vals_t = jnp.concatenate([kv[i, p, 1] for i in blocks[b]] + [gkv[p, 1]], axis=1)
            e = jnp.exp(s_ref[b] - m_ref[b])
            scale = 1.0 / jnp.sum(e, axis=0, keepdims=True)
            o = jnp.dot(vals_t, e.astype(BF16), preferred_element_type=F32) * scale
            c = jnp.concatenate([o[:64, :BLOCK], o[64:, BLOCK:]], axis=0).astype(BF16)
            pctx[b * 32:(b + 1) * 32, kcols] = lax.dot_general(
                pool, c, (((1,), (1,)), ((), ())), preferred_element_type=F32)

    def two_pairs(i, carry):
        score(2 * i + 1, s_b, m_b)
        combine(2 * i, s_a, m_a)
        score(jnp.minimum(2 * i + 2, pairs - 1), s_a, m_a)
        combine(2 * i + 1, s_b, m_b)
        return carry

    score(0, s_a, m_a)
    lax.fori_loop(0, pairs // 2, two_pairs, 0)
    got_out.wait()
    rows = pctx.shape[0]
    upper = pctx[...].astype(BF16)
    lower = (pctx[...] - upper.astype(F32)).astype(BF16)
    both = jnp.concatenate([upper, lower], axis=0)
    for n in range(width // 256):
        made = jnp.dot(both, wout_v[:, n * 256:(n + 1) * 256], preferred_element_type=F32)
        proj[:, n * 256:(n + 1) * 256] = made[:rows] + made[rows:]
    pooled = proj[...]
    centered = pooled - jnp.mean(pooled, axis=1, keepdims=True)
    var = jnp.mean(centered * centered, axis=1, keepdims=True)
    normed = centered * lax.rsqrt(var + 1e-05) * gain[...].reshape(1, width)
    row_block = first + lax.broadcasted_iota(jnp.int32, (rows, width), 0) * POOL // BLOCK
    out[...] = jnp.where(row_block < live, normed, 0.0).astype(BF16)
    for copy in sends:
        copy.wait_send()
    for pair in passed:
        for block in pair:
            def sent(n, carry, block=block):
                pass_on(block, n).wait_send()
                return carry

            lax.fori_loop(0, width // TILE, sent, 0)


def body(shards, frames, w_query, w_kv, w_out, norm_gain, rand_owner, rand_slot, global_pos, length):
    local_rows, width = frames.shape
    assert local_rows == 2 * BLOCK and width == HEADS * 64 and global_pos.shape[0] == BLOCK
    hbm = pl.BlockSpec(memory_space=pl.ANY)
    vmem = pl.BlockSpec(memory_space=pltpu.VMEM)
    smem = pl.BlockSpec(memory_space=pltpu.SMEM)
    keys = (4 + rand_owner.shape[1]) * BLOCK
    n_sends = 6 if shards == 8 else 2 * (shards - 1)
    return pl.pallas_call(
        functools.partial(kernel, shards),
        out_shape=jax.ShapeDtypeStruct((local_rows // POOL, width), BF16),
        in_specs=[hbm, hbm, hbm, hbm, vmem, smem, smem, vmem, smem],
        out_specs=vmem,
        scratch_shapes=[
            pltpu.VMEM((shards, 2, BLOCK, width), BF16),
            pltpu.VMEM((2 * shards, width // 128, 2, BLOCK, BLOCK), BF16),
            pltpu.VMEM((width, width), BF16),
            pltpu.VMEM((width, 2 * width), BF16),
            pltpu.VMEM((width, width), BF16),
            pltpu.VMEM((local_rows, width), BF16),
            pltpu.VMEM((width // 128, 2, BLOCK, BLOCK), F32),
            pltpu.VMEM((width // 128, 2, BLOCK, BLOCK), BF16),
            pltpu.VMEM((local_rows // POOL, width), F32),
            pltpu.VMEM((local_rows // POOL, width), F32),
            pltpu.VMEM((2, keys, 2 * BLOCK), F32),
            pltpu.VMEM((2, keys, 2 * BLOCK), F32),
            pltpu.VMEM((2, 1, 2 * BLOCK), F32),
            pltpu.VMEM((2, 1, 2 * BLOCK), F32),
            pltpu.SemaphoreType.DMA((4,)),
            pltpu.SemaphoreType.DMA((n_sends,)),
            pltpu.SemaphoreType.DMA((shards, 2)),
            pltpu.SemaphoreType.DMA((2 * shards, width // TILE)),
            pltpu.SemaphoreType.DMA((2 * shards, width // TILE)),
        ],
        compiler_params=pltpu.CompilerParams(
            collective_id=0, has_side_effects=True, vmem_limit_bytes=60 * 1024 * 1024),
        cost_estimate=pl.CostEstimate(
            flops=20_000_000_000, bytes_accessed=20_000_000, transcendentals=5_000_000),
    )(frames.reshape(2, BLOCK, width), w_query, w_kv, w_out, norm_gain,
      rand_owner, rand_slot, global_pos.reshape(1, BLOCK), length)


def solution(mesh):
    placed = (
        P(("rec", "tm"), None), P(), P(), P(), P(),
        P(("rec", "tm"), None), P(("rec", "tm"), None), P("rec"), P("rec"),
    )
    return jax.shard_map(
        functools.partial(body, mesh.shape["tm"]), mesh=mesh, in_specs=placed,
        out_specs=P(("rec", "tm"), None), check_vma=False)
```

```python
import functools

import jax
import jax.numpy as jnp
from jax import lax
from jax.experimental import pallas as pl
from jax.experimental.pallas import tpu as pltpu
from jax.sharding import PartitionSpec as P

HEADS = 20
BLOCK = 128
POOL = 4
TILE = 256
MESH = pl.DeviceIdType.MESH
F32 = jnp.float32
BF16 = jnp.bfloat16


def kernel(shards, frames, w_query, w_kv, w_out, gain, owner, slot, gpos, length, out,
           fall, kv, wq_v, wkv_v, wout_v, q_v, gacc, gkv, pctx, proj, s_a, s_b, m_a, m_b, lsem, ssem, rsem, kssem, krsem):
    me = lax.axis_index("tm")
    width = wq_v.shape[0]
    picks = owner.shape[1]
    first = me * 2
    count = [0]
    sends = []

    def local(src, dst, index):
        copy = pltpu.make_async_copy(src, dst, lsem.at[index])
        copy.start()
        return copy

    def send(src, shard, part, target):
        copy = pltpu.make_async_remote_copy(
            src_ref=src, dst_ref=fall.at[shard, part], send_sem=ssem.at[count[0]],
            recv_sem=rsem.at[shard, part], device_id={"tm": target}, device_id_type=MESH)
        count[0] += 1
        copy.start()
        sends.append(copy)

    def arrived(shard, part):
        pltpu.make_async_copy(fall.at[shard, part], fall.at[shard, part],
                              rsem.at[shard, part]).wait()

    own = local(frames, fall.at[me], 0)
    got_q = local(w_query, wq_v, 1)
    got_kv = local(w_kv, wkv_v, 2)
    got_out = local(w_out, wout_v, 3)

    if shards == 8:
        side = me + 1 - 2 * (me % 2)
        near_x = me + 2 - 4 * ((me // 2) % 2)
        near_y = (me + 4) % 8
        partners = [side, near_x, near_y]
    else:
        partners = [(me + k) % shards for k in range(1, shards)]
    barrier = pltpu.get_barrier_semaphore()
    for target in partners:
        pl.semaphore_signal(barrier, inc=1, device_id={"tm": target}, device_id_type=MESH)
    pl.semaphore_wait(barrier, len(partners))
    if shards == 8:
        send(frames.at[0], me, 0, near_x)
        send(frames.at[1], me, 1, near_y)
        send(frames.at[1], me, 1, near_x)
        send(frames.at[0], me, 0, near_y)
    else:
        for target in partners:
            send(frames.at[0], me, 0, target)
            send(frames.at[1], me, 1, target)

    gacc[...] = jnp.zeros_like(gacc)
    pos_t = jnp.broadcast_to(gpos[...], (BLOCK, BLOCK)).T
    lane = lax.broadcasted_iota(jnp.int32, (BLOCK, BLOCK), 1)

    def onehot(block):
        return jnp.where(pos_t == block * BLOCK + lane, 1.0, 0.0).astype(BF16)

    passed = []

    def pass_on(block, n):
        part = kv.at[block, pl.ds(n * 2, 2)]
        return pltpu.make_async_remote_copy(
            src_ref=part, dst_ref=part, send_sem=kssem.at[block, n], recv_sem=krsem.at[block, n],
            device_id={"tm": side}, device_id_type=MESH)

    def add_global(n, hot, keys, vals_t):
        far_k = jnp.dot(hot, keys, preferred_element_type=F32)
        far_v = lax.dot_general(vals_t, hot, (((1,), (1,)), ((), ())), preferred_element_type=F32)
        for j in range(2):
            gacc[n * 2 + j, 0] += far_k[:, j * 128:(j + 1) * 128]
            gacc[n * 2 + j, 1] += far_v[j * 128:(j + 1) * 128]

    def project(shard_a, part_a, shard_b, part_b):
        block_a, block_b = shard_a * 2 + part_a, shard_b * 2 + part_b
        hot = jnp.concatenate([onehot(block_a), onehot(block_b)], axis=1)

        def step(n, carry):
            kcols = pl.ds(pl.multiple_of(n * TILE, TILE), TILE)
            vcols = pl.ds(pl.multiple_of(width + n * TILE, TILE), TILE)
            rows = jnp.concatenate([fall[shard_a, part_a], fall[shard_b, part_b]], axis=0)
            keys = jnp.dot(rows, wkv_v[:, kcols], preferred_element_type=F32).astype(BF16)
            vals_t = jnp.dot(rows, wkv_v[:, vcols], preferred_element_type=F32).T.astype(BF16)
            for k, block in enumerate((block_a, block_b)):
                for j in range(2):
                    kv[block, n * 2 + j, 0] = keys[k * 128:(k + 1) * 128, j * 128:(j + 1) * 128]
                    kv[block, n * 2 + j, 1] = vals_t[j * 128:(j + 1) * 128, k * 128:(k + 1) * 128]
            if shards == 8:
                pass_on(block_a, n).start()
                pass_on(block_b, n).start()
            add_global(n, hot, keys, vals_t)
            return carry

        lax.fori_loop(0, width // TILE, step, 0, unroll=shards == 8)
        if shards == 8:
            passed.append((block_a, block_b))

    def take(shard_a, part_a, shard_b, part_b):
        block_a, block_b = shard_a * 2 + part_a, shard_b * 2 + part_b
        hot = jnp.concatenate([onehot(block_a), onehot(block_b)], axis=1)

        def step(n, carry):
            pass_on(block_a, n).wait_recv()
            pass_on(block_b, n).wait_recv()
            keys = jnp.concatenate([jnp.concatenate(
                [kv[block, n * 2 + j, 0] for j in range(2)], axis=1)
                for block in (block_a, block_b)], axis=0)
            vals_t = jnp.concatenate([jnp.concatenate(
                [kv[block, n * 2 + j, 1] for block in (block_a, block_b)], axis=1)
                for j in range(2)], axis=0)
            add_global(n, hot, keys, vals_t)
            return carry

        lax.fori_loop(0, width // TILE, step, 0)

    own.wait()
    got_q.wait()

    def query_step(n, carry):
        cols = pl.ds(pl.multiple_of(n * 256, 256), 256)
        rows = jnp.concatenate([fall[me, 0], fall[me, 1]], axis=0)
        made = jnp.dot(rows, wq_v[:, cols], preferred_element_type=F32).astype(BF16)
        q_v[:, cols] = (made.astype(F32) * 0.125).astype(BF16)
        return carry

    lax.fori_loop(0, width // 256, query_step, 0)
    got_kv.wait()
    project(me, 0, me, 1)
    if shards == 8:
        diag = near_x + near_y - me
        side_x, side_y = (v + 1 - 2 * (v % 2) for v in (near_x, near_y))
        side_d = diag + 1 - 2 * (diag % 2)
        arrived(near_x, 0)
        send(fall.at[near_x, 0], near_x, 0, near_y)
        arrived(near_y, 1)
        send(fall.at[near_y, 1], near_y, 1, near_x)
        project(near_x, 0, near_y, 1)
        take(side, 0, side, 1)
        take(side_x, 0, side_y, 1)
        arrived(near_x, 1)
        arrived(near_y, 0)
        project(near_x, 1, near_y, 0)
        take(side_x, 1, side_y, 0)
        arrived(diag, 0)
        arrived(diag, 1)
        project(diag, 0, diag, 1)
        take(side_d, 0, side_d, 1)
    else:
        for k in range(1, shards):
            source = (me + shards - k) % shards
            arrived(source, 0)
            arrived(source, 1)
            project(source, 0, source, 1)
    gkv[...] = gacc[...].astype(BF16)

    live = length[0]
    low = jnp.where(lane < 64, 1.0, 0.0).astype(BF16)
    high = jnp.where(lane < 64, 0.0, 1.0).astype(BF16)
    pool_row = lax.broadcasted_iota(jnp.int32, (BLOCK // POOL, BLOCK), 0)
    pool_col = lax.broadcasted_iota(jnp.int32, (BLOCK // POOL, BLOCK), 1)
    pool = jnp.where(pool_col // POOL == pool_row, 1.0 / POOL, 0.0).astype(BF16)
    far = jnp.where(pos_t >= live * BLOCK, -1e30, 0.0)
    far = jnp.concatenate([far, far], axis=1)
    blocks, biases = [], []
    for b in range(2):
        ids = [first + b - 1 + k for k in range(3)]
        ids += [owner[b, j] * 2 + slot[b, j] for j in range(picks)]
        blocks.append([jnp.clip(i, 0, 2 * shards - 1) for i in ids])
        biases.append([jnp.where((i >= 0) & (i < live), 0.0, -1e30) for i in ids])

    pairs = width // 128

    def score(p, s_ref, m_ref):
        kcols = pl.ds(pl.multiple_of(p * 128, 128), 128)
        for b in range(2):
            q = q_v[b * BLOCK:(b + 1) * BLOCK, kcols]
            qs = jnp.concatenate([q * low, q * high], axis=0)
            keys = jnp.concatenate([kv[i, p, 0] for i in blocks[b]] + [gkv[p, 0]], axis=0)
            s = lax.dot_general(keys, qs, (((1,), (1,)), ((), ())), preferred_element_type=F32)
            near = [s[k * BLOCK:(k + 1) * BLOCK] + bias for k, bias in enumerate(biases[b])]
            s = jnp.concatenate(near + [s[len(near) * BLOCK:] + far], axis=0)
            s_ref[b] = s
            m_ref[b] = jnp.max(s, axis=0, keepdims=True)

    def combine(p, s_ref, m_ref):
        kcols = pl.ds(pl.multiple_of(p * 128, 128), 128)
        for b in range(2):
            vals_t = jnp.concatenate([kv[i, p, 1] for i in blocks[b]] + [gkv[p, 1]], axis=1)
            e = jnp.exp(s_ref[b] - m_ref[b])
            scale = 1.0 / jnp.sum(e, axis=0, keepdims=True)
            o = jnp.dot(vals_t, e.astype(BF16), preferred_element_type=F32) * scale
            c = jnp.concatenate([o[:64, :BLOCK], o[64:, BLOCK:]], axis=0).astype(BF16)
            pctx[b * 32:(b + 1) * 32, kcols] = lax.dot_general(
                pool, c, (((1,), (1,)), ((), ())), preferred_element_type=F32)

    def two_pairs(i, carry):
        score(2 * i + 1, s_b, m_b)
        combine(2 * i, s_a, m_a)
        score(jnp.minimum(2 * i + 2, pairs - 1), s_a, m_a)
        combine(2 * i + 1, s_b, m_b)
        return carry

    score(0, s_a, m_a)
    lax.fori_loop(0, pairs // 2, two_pairs, 0)
    got_out.wait()
    rows = pctx.shape[0]
    upper = pctx[...].astype(BF16)
    lower = (pctx[...] - upper.astype(F32)).astype(BF16)
    both = jnp.concatenate([upper, lower], axis=0)
    for n in range(width // 256):
        made = jnp.dot(both, wout_v[:, n * 256:(n + 1) * 256], preferred_element_type=F32)
        proj[:, n * 256:(n + 1) * 256] = made[:rows] + made[rows:]
    pooled = proj[...]
    centered = pooled - jnp.mean(pooled, axis=1, keepdims=True)
    var = jnp.mean(centered * centered, axis=1, keepdims=True)
    normed = centered * lax.rsqrt(var + 1e-05) * gain[...].reshape(1, width)
    row_block = first + lax.broadcasted_iota(jnp.int32, (rows, width), 0) * POOL // BLOCK
    out[...] = jnp.where(row_block < live, normed, 0.0).astype(BF16)
    for copy in sends:
        copy.wait_send()
    for pair in passed:
        for block in pair:
            def sent(n, carry, block=block):
                pass_on(block, n).wait_send()
                return carry

            lax.fori_loop(0, width // TILE, sent, 0)


def body(shards, frames, w_query, w_kv, w_out, norm_gain, rand_owner, rand_slot, global_pos, length):
    local_rows, width = frames.shape
    assert local_rows == 2 * BLOCK and width == HEADS * 64 and global_pos.shape[0] == BLOCK
    hbm = pl.BlockSpec(memory_space=pl.ANY)
    vmem = pl.BlockSpec(memory_space=pltpu.VMEM)
    smem = pl.BlockSpec(memory_space=pltpu.SMEM)
    keys = (4 + rand_owner.shape[1]) * BLOCK
    n_sends = 6 if shards == 8 else 2 * (shards - 1)
    return pl.pallas_call(
        functools.partial(kernel, shards),
        out_shape=jax.ShapeDtypeStruct((local_rows // POOL, width), BF16),
        in_specs=[hbm, hbm, hbm, hbm, vmem, smem, smem, vmem, smem],
        out_specs=vmem,
        scratch_shapes=[
            pltpu.VMEM((shards, 2, BLOCK, width), BF16),
            pltpu.VMEM((2 * shards, width // 128, 2, BLOCK, BLOCK), BF16),
            pltpu.VMEM((width, width), BF16),
            pltpu.VMEM((width, 2 * width), BF16),
            pltpu.VMEM((width, width), BF16),
            pltpu.VMEM((local_rows, width), BF16),
            pltpu.VMEM((width // 128, 2, BLOCK, BLOCK), F32),
            pltpu.VMEM((width // 128, 2, BLOCK, BLOCK), BF16),
            pltpu.VMEM((local_rows // POOL, width), F32),
            pltpu.VMEM((local_rows // POOL, width), F32),
            pltpu.VMEM((2, keys, 2 * BLOCK), F32),
            pltpu.VMEM((2, keys, 2 * BLOCK), F32),
            pltpu.VMEM((2, 1, 2 * BLOCK), F32),
            pltpu.VMEM((2, 1, 2 * BLOCK), F32),
            pltpu.SemaphoreType.DMA((4,)),
            pltpu.SemaphoreType.DMA((n_sends,)),
            pltpu.SemaphoreType.DMA((shards, 2)),
            pltpu.SemaphoreType.DMA((2 * shards, width // TILE)),
            pltpu.SemaphoreType.DMA((2 * shards, width // TILE)),
        ],
        compiler_params=pltpu.CompilerParams(
            collective_id=0, has_side_effects=True, vmem_limit_bytes=60 * 1024 * 1024),
        cost_estimate=pl.CostEstimate(
            flops=20_000_000_000, bytes_accessed=20_000_000, transcendentals=5_000_000),
    )(frames.reshape(2, BLOCK, width), w_query, w_kv, w_out, norm_gain,
      rand_owner, rand_slot, global_pos.reshape(1, BLOCK), length)


def solution(mesh):
    placed = (
        P(("rec", "tm"), None), P(), P(), P(), P(),
        P(("rec", "tm"), None), P(("rec", "tm"), None), P("rec"), P("rec"),
    )
    return jax.shard_map(
        functools.partial(body, mesh.shape["tm"]), mesh=mesh, in_specs=placed,
        out_specs=P(("rec", "tm"), None), check_vma=False)
```
